32 devices in a mesh: lev: 2 (over y), hor: 16 (over z, x, core).
Axes of the slice: x: 2, y: 2, z: 4, core: 2. Of those that a mesh axis runs over, the one named last changes fastest.
Arguments:
- heat_field: float32 [64, 512, 512], P('lev', 'hor'), may hold values from -6 to 6
- saline_field: float32 [64, 512, 512], P('lev', 'hor'), may hold values from -6 to 6
- updraft_speed: float32 [64, 512, 512], P('lev', 'hor'), may hold values from -3 to 3
- heat_mixing_rates: float32 [64], P('lev'), may hold values from 0.05 to 1
- saline_mixing_rates: float32 [64], P('lev'), may hold values from 0.05 to 1
- cross_mixing_rates: float32 [64], P('lev'), may hold values from 0.2 to 1
Outputs:
- updated_heat_field: float32 [64, 512, 512], P('lev', 'hor')
- salt_out: float32 [64, 512, 512], P('lev', 'hor')
The draws below stay inside these ranges and needn't reach their ends.
All inputs are finite; a program needn't handle non-finite values.
Results may differ from the reference program's by a relative error of at most 0.000073.
Values sent between devices are 32-bit elements; how exact they have to be, the bound alone decides.
A program may use at most 128 MiB of HBM per device.

```python
import math
import jax
import jax.numpy as jnp
from jax import lax

GRID_WIDTH_EAST = 512
GRID_WIDTH_NORTH = 512
DEPTH_LAYERS = 64


def shard_levels(own_key, shape, shards, least, largest):
    factor_of = 1.0
    for axis_at, blocks in shards:
        draws = jax.random.uniform(jax.random.fold_in(jax.random.fold_in(own_key, 6), axis_at), (blocks,), jnp.float32, least / len(shards), largest / len(shards))
        factor_of = factor_of * jnp.repeat(jnp.exp(draws), shape[axis_at] // blocks).reshape((-1,) + (1,) * (len(shape) - 1 - axis_at))
    return factor_of


def gaussian(key, shape, scale, reach, split=(), kind=jnp.bfloat16):
    entries = scale * jax.random.normal(key, shape, jnp.float32)
    if split:
        entries = entries * shard_levels(key, shape, split, -0.22, 0.18)
    return jnp.clip(entries, -reach, reach).astype(kind)


def setup_inputs(seed: int = 0) -> dict:
    key_list = jax.random.split(jax.random.key(seed), 7)
    heat_field = gaussian(key_list[0], (DEPTH_LAYERS, GRID_WIDTH_EAST, GRID_WIDTH_NORTH), 1.0, 6.0, ((0, 2), (1, 16)), jnp.float32)
    saline_field = gaussian(key_list[1], (DEPTH_LAYERS, GRID_WIDTH_EAST, GRID_WIDTH_NORTH), 1.0, 6.0, ((0, 2), (1, 16)), jnp.float32)
    updraft_speed = gaussian(key_list[2], (DEPTH_LAYERS, GRID_WIDTH_EAST, GRID_WIDTH_NORTH), 0.5, 3.0, ((0, 2), (1, 16)), jnp.float32)
    heat_mixing_rates = jnp.clip(jnp.exp(math.log(1.0) - 2.9957323 * jax.random.uniform(key_list[3], (DEPTH_LAYERS,), jnp.float32) ** shard_levels(key_list[3], (DEPTH_LAYERS,), ((0, 2),), -0.2, 0.2)), 0.05, 1.0)
    saline_mixing_rates = jnp.clip(jnp.exp(math.log(1.0) - 2.9957323 * jax.random.uniform(key_list[4], (DEPTH_LAYERS,), jnp.float32) ** shard_levels(key_list[4], (DEPTH_LAYERS,), ((0, 2),), -0.2, 0.2)), 0.05, 1.0)
    cross_mixing_rates = jnp.clip(jnp.exp(math.log(1.0) - 1.609438 * jax.random.uniform(key_list[5], (DEPTH_LAYERS,), jnp.float32) ** shard_levels(key_list[5], (DEPTH_LAYERS,), ((0, 2),), -0.2, 0.2)), 0.2, 1.0)
    return dict(heat_field=heat_field, saline_field=saline_field, updraft_speed=updraft_speed, heat_mixing_rates=heat_mixing_rates, saline_mixing_rates=saline_mixing_rates, cross_mixing_rates=cross_mixing_rates)


def signed_waves(length):
    waves = jnp.arange(length)
    return jnp.where(waves < length // 2, waves, waves - length)


def layer_fourier_modes(pieces):
    temp_level, salt_level, diff_temp, diff_salt, cross_rate = pieces
    wave_x = signed_waves(GRID_WIDTH_EAST).astype(temp_level.dtype)
    wave_y = signed_waves(GRID_WIDTH_NORTH).astype(temp_level.dtype)
    modulus = (wave_x[:, None] * wave_x[:, None] + wave_y[None, :] * wave_y[None, :]) / ((GRID_WIDTH_EAST / 2.0) * (GRID_WIDTH_EAST / 2.0))
    fourier_temp = jnp.fft.fft2(temp_level)
    fourier_salt = jnp.fft.fft2(salt_level)
    diag_temp = 1.0 + diff_temp * modulus
    diag_salt = 1.0 + diff_salt * modulus
    cross_term = cross_rate * modulus
    determinant = diag_temp * diag_salt + cross_term * cross_term
    new_temp = (diag_salt * fourier_temp - cross_term * fourier_salt) / determinant
    new_salt = (diag_temp * fourier_salt + cross_term * fourier_temp) / determinant
    back_temp = jnp.real(jnp.fft.ifft2(new_temp)).astype(temp_level.dtype)
    back_salt = jnp.real(jnp.fft.ifft2(new_salt)).astype(temp_level.dtype)
    return back_temp, back_salt


def reference(heat_field, saline_field, updraft_speed, heat_mixing_rates, saline_mixing_rates, cross_mixing_rates):
    filtered_heat_field, filtered_saline_field = lax.map(layer_fourier_modes, (heat_field, saline_field, heat_mixing_rates, saline_mixing_rates, cross_mixing_rates))
    interface_flow = 0.5 * (updraft_speed[:-1] + updraft_speed[1:]) + 0.5 * 0.5 * ((filtered_heat_field[:-1] + filtered_heat_field[1:]) - (filtered_saline_field[:-1] + filtered_saline_field[1:]))
    upward_flow = jnp.maximum(interface_flow, 0.0)
    downward_flow = jnp.minimum(interface_flow, 0.0)
    heat_transport = upward_flow * filtered_heat_field[:-1] + downward_flow * filtered_heat_field[1:]
    flux_salt = upward_flow * filtered_saline_field[:-1] + downward_flow * filtered_saline_field[1:]
    zero_face = jnp.zeros_like(heat_transport[:1])
    heat_transport = jnp.concatenate([zero_face, heat_transport, zero_face], axis=0)
    flux_salt = jnp.concatenate([zero_face, flux_salt, zero_face], axis=0)
    updated_heat_field = filtered_heat_field - 0.25 * (heat_transport[1:] - heat_transport[:-1])
    salt_out = filtered_saline_field - 0.25 * (flux_salt[1:] - flux_salt[:-1])
    return updated_heat_field, salt_out
```

```python
import functools
import math

import jax
import jax.numpy as jnp
import ml_dtypes
import numpy as np
from jax import lax
from jax.experimental import pallas as pl
from jax.experimental.pallas import tpu as pltpu
from jax.sharding import PartitionSpec as P

MESH = pl.DeviceIdType.MESH
LANES = 128
buoyancy = 0.5
advective_number = 0.25


def wave_table(length):
    half = length // 2
    waves = []
    for parity in range(2):
        k = np.repeat(2 * np.arange(half // 2) + parity, 2)
        if parity == 0:
            k[1] = half
        waves.append(k)
    return waves


def basis(length):
    half = length // 2
    points = np.arange(half)
    out = []
    for parity, k in enumerate(wave_table(length)):
        angle = 2.0 * math.pi / length * ((k[:, None] * points[None, :]) % length)
        rows = np.where(np.arange(half)[:, None] % 2 == 0, np.cos(angle), np.sin(angle))
        rows = rows * math.sqrt(2.0 / length)
        if parity == 0:
            rows[0] = 1.0 / math.sqrt(length)
            rows[1] = np.cos(math.pi * points) / math.sqrt(length)
        out.append(rows)
    return out


def thirds(matrix, axis):
    high = matrix.astype(ml_dtypes.bfloat16)
    low = (matrix - high.astype(np.float64)).astype(ml_dtypes.bfloat16)
    return np.concatenate([high, high, low], axis=axis)


def split3(x, axis):
    high = x.astype(jnp.bfloat16)
    low = (x - high.astype(jnp.float32)).astype(jnp.bfloat16)
    return jnp.concatenate([high, low, high], axis=axis)


def dot(a, b):
    return jnp.dot(a, b, preferred_element_type=jnp.float32)


def block_transpose(tiles, width, lane):
    count = len(tiles)
    tiles = list(tiles)
    step = count // 2
    while step >= 1:
        keep = (lane // width) % (2 * step) < step
        for i in range(count):
            if i & step == 0:
                a, b = tiles[i], tiles[i + step]
                tiles[i] = jnp.where(keep, a, pltpu.roll(b, step * width, 1))
                tiles[i + step] = jnp.where(
                    keep, pltpu.roll(a, LANES - step * width, 1), b
                )
        step //= 2
    return tiles


def kernel(
    parts, levs, slots,
    heat, salt, speed, rate_t, rate_s, rate_c, fwd_y, inv_y, fwd_x, inv_x, wx2, wy2,
    out_t, out_s,
    send, recv, back_send, back_recv, ext,
    send_sem, recv_sem, back_send_sem, back_recv_sem, speed_sem, halo_send, halo_recv,
):
    layers, rows, length_y = heat.shape
    pack = LANES // slots
    chunks = layers // pack
    half_y = length_y // 2
    length_x = rows * parts
    half_x = length_x // 2
    me = lax.axis_index("hor")
    lev = lax.axis_index("lev")
    has_low = lev > 0
    has_high = lev < levs - 1

    def peer(d):
        return lax.rem(me + d, parts)

    barrier = pltpu.get_barrier_semaphore()

    def greet(d, carry):
        pl.semaphore_signal(barrier, inc=1, device_id={"hor": peer(d)}, device_id_type=MESH)
        return carry

    lax.fori_loop(1, parts, greet, 0)

    @pl.when(has_low)
    def _():
        pl.semaphore_signal(barrier, inc=1, device_id={"lev": lev - 1}, device_id_type=MESH)

    @pl.when(has_high)
    def _():
        pl.semaphore_signal(barrier, inc=1, device_id={"lev": lev + 1}, device_id_type=MESH)

    speed_copy = pltpu.make_async_copy(speed, ext.at[2, pl.ds(1, layers)], speed_sem)
    speed_copy.start()

    def halo_up(kind):
        first, count = (2, 1) if kind == 0 else (0, 2)
        return pltpu.make_async_remote_copy(
            src_ref=ext.at[pl.ds(first, count), layers],
            dst_ref=ext.at[pl.ds(first, count), 0],
            send_sem=halo_send.at[0, kind],
            recv_sem=halo_recv.at[0, kind],
            device_id={"lev": lev + 1},
            device_id_type=MESH,
        )

    def halo_down(kind):
        first, count = (2, 1) if kind == 0 else (0, 2)
        return pltpu.make_async_remote_copy(
            src_ref=ext.at[pl.ds(first, count), 1],
            dst_ref=ext.at[pl.ds(first, count), layers + 1],
            send_sem=halo_send.at[1, kind],
            recv_sem=halo_recv.at[1, kind],
            device_id={"lev": lev - 1},
            device_id_type=MESH,
        )

    def send_halo(kind):
        @pl.when(has_high)
        def _():
            halo_up(kind).start()

        @pl.when(has_low)
        def _():
            halo_down(kind).start()

    def wait_halo(kind):
        @pl.when(has_high)
        def _():
            halo_up(kind).wait_send()
            halo_down(kind).wait_recv()

        @pl.when(has_low)
        def _():
            halo_down(kind).wait_send()
            halo_up(kind).wait_recv()

    @pl.when(jnp.logical_not(has_low))
    def _():
        ext[:, 0] = jnp.zeros((3, rows, length_y), jnp.float32)

    @pl.when(jnp.logical_not(has_high))
    def _():
        ext[:, layers + 1] = jnp.zeros((3, rows, length_y), jnp.float32)

    def chunk_of(i):
        return lax.rem(i + chunks - 1, chunks)

    def lane_of(shape):
        return lax.broadcasted_iota(jnp.int32, shape, 1)

    def exchange(source, target, s_sem, r_sem, c):
        def one(d, carry):
            q = peer(d)
            pltpu.make_async_remote_copy(
                src_ref=source.at[c, q],
                dst_ref=target.at[c, me],
                send_sem=s_sem.at[c],
                recv_sem=r_sem.at[c],
                device_id={"hor": q},
                device_id_type=MESH,
            ).start()
            return carry

        lax.fori_loop(1, parts, one, 0)
        target[c, me] = source[c, me]

    def wait_all(ref, sem, c):
        view = ref.at[c, pl.ds(0, parts - 1)]
        pltpu.make_async_copy(view, view, sem.at[c]).wait()

    def north(c):
        level = pl.ds(c * pack, pack)
        x = jnp.concatenate(
            [ref[level].reshape(pack * rows, length_y) for ref in (heat, salt)], axis=0
        )
        a, b = x[:, :half_y], x[:, half_y:]
        spectra = [
            dot(split3(a + b, 1), fwd_y[0]).reshape(2, pack, rows, half_y),
            dot(split3(a - b, 1), fwd_y[1]).reshape(2, pack, rows, half_y),
        ]
        lane = lane_of((rows, LANES))
        for parity in range(2):
            for tile in range(half_y // LANES):
                q0 = (parity * (half_y // LANES) + tile) * pack
                cols = slice(tile * LANES, (tile + 1) * LANES)
                for f in range(2):
                    tiles = [spectra[parity][f, z, :, cols] for z in range(pack)]
                    for i, t in enumerate(block_transpose(tiles, slots, lane)):
                        send[c, q0 + i, f] = t

    def east(c):
        both = jnp.concatenate(
            [recv[c, :, f].reshape(length_x, LANES) for f in range(2)], axis=1
        )
        a, b = both[:half_x], both[half_x:]
        block = lane_of((1, LANES)) // slots
        rates = []
        for ref in (rate_t, rate_s, rate_c):
            row = jnp.full((1, LANES), ref[c * pack], jnp.float32)
            for z in range(1, pack):
                row = jnp.where(block == z, ref[c * pack + z], row)
            rates.append(row)
        waves_y = wy2[me]
        result = []
        for parity, x in enumerate((a + b, a - b)):
            spec = dot(fwd_x[parity], split3(x, 0))
            t, s = spec[:, :LANES], spec[:, LANES:]
            modulus = wx2[parity] + waves_y
            diag_t = 1.0 + rates[0] * modulus
            diag_s = 1.0 + rates[1] * modulus
            cross = rates[2] * modulus
            inverse = 1.0 / (diag_t * diag_s + cross * cross)
            new = jnp.concatenate(
                [(diag_s * t - cross * s) * inverse, (diag_t * s + cross * t) * inverse], axis=1
            )
            result.append(dot(inv_x[parity], split3(new, 0)))
        for k, x in enumerate((result[0] + result[1], result[0] - result[1])):
            for f in range(2):
                back_send[c, pl.ds(k * (parts // 2), parts // 2), f] = x[
                    :, f * LANES : (f + 1) * LANES
                ].reshape(parts // 2, rows, LANES)

    def south(c):
        lane = lane_of((rows, LANES))
        ends = []
        for parity in range(2):
            fields = []
            columns = []
            for f in range(2):
                by_tile = []
                for tile in range(half_y // LANES):
                    q0 = (parity * (half_y // LANES) + tile) * pack
                    tiles = [back_recv[c, q0 + i, f] for i in range(pack)]
                    by_tile.append(block_transpose(tiles, slots, lane))
                for z in range(pack):
                    columns.append(jnp.concatenate([t[z] for t in by_tile], axis=1))
            x = jnp.concatenate(columns, axis=0)
            ends.append(dot(split3(x, 1), inv_y[parity]))
        for k, x in enumerate((ends[0] + ends[1], ends[0] - ends[1])):
            ext[pl.ds(0, 2), pl.ds(1 + c * pack, pack), :, pl.ds(k * half_y, half_y)] = x.reshape(
                2, pack, rows, half_y
            )

    def advect(c):
        base = c * pack

        def face(j, r):
            low_t, high_t = ext[0, j, r], ext[0, j + 1, r]
            low_s, high_s = ext[1, j, r], ext[1, j + 1, r]
            flow = 0.5 * (ext[2, j, r] + ext[2, j + 1, r]) + buoyancy * 0.5 * (
                (low_t + high_t) - (low_s + high_s)
            )
            shut = jnp.logical_or(
                jnp.logical_and(j == 0, jnp.logical_not(has_low)),
                jnp.logical_and(j == layers, jnp.logical_not(has_high)),
            )
            flow = flow * jnp.where(shut, 0.0, 1.0)
            up = jnp.maximum(flow, 0.0)
            down = jnp.minimum(flow, 0.0)
            return up * low_t + down * high_t, up * low_s + down * high_s

        for group in range(rows // 8):
            r = pl.ds(group * 8, 8)
            below = face(base, r)
            for z in range(pack):
                level = base + z
                above = face(level + 1, r)
                out_t[level, r] = ext[0, level + 1, r] - advective_number * (above[0] - below[0])
                out_s[level, r] = ext[1, level + 1, r] - advective_number * (above[1] - below[1])
                below = above

    c0 = chunk_of(0)
    north(c0)
    pl.semaphore_wait(
        barrier, parts - 1 + jnp.where(has_low, 1, 0) + jnp.where(has_high, 1, 0)
    )
    exchange(send, recv, send_sem, recv_sem, c0)

    def forward(i, carry):
        c = chunk_of(i)
        north(c)
        exchange(send, recv, send_sem, recv_sem, c)
        return carry

    lax.fori_loop(1, chunks, forward, 0)
    speed_copy.wait()
    send_halo(0)

    def middle(i, carry):
        c = chunk_of(i)
        wait_all(recv, recv_sem, c)
        east(c)
        exchange(back_send, back_recv, back_send_sem, back_recv_sem, c)
        return carry

    lax.fori_loop(0, chunks, middle, 0)

    def backward(i, carry):
        c = chunk_of(i)
        wait_all(back_recv, back_recv_sem, c)
        south(c)

        @pl.when(i == 1)
        def _():
            send_halo(1)

        @pl.when(i == 2)
        def _():
            wait_halo(0)
            wait_halo(1)

        @pl.when(i >= 2)
        def _():
            advect(c - 1)

        return carry

    lax.fori_loop(0, chunks, backward, 0)
    advect(chunks - 2)
    advect(chunks - 1)

    def drain(c, carry):
        wait_all(send, send_sem, c)
        wait_all(back_send, back_send_sem, c)
        return carry

    lax.fori_loop(0, chunks, drain, 0)


def shards(heat, salt, speed, rate_t, rate_s, rate_c):
    layers, rows, length_y = heat.shape
    parts = lax.axis_size("hor")
    levs = lax.axis_size("lev")
    length_x = rows * parts
    slots = length_y // parts
    pack = LANES // slots
    chunks = layers // pack
    rows_y, rows_x = basis(length_y), basis(length_x)
    fwd_y = np.stack([thirds(m.T, 0) for m in rows_y])
    inv_y = np.stack([thirds(m, 0) for m in rows_y])
    fwd_x = np.stack([thirds(m, 1) for m in rows_x])
    inv_x = np.stack([thirds(m.T, 1) for m in rows_x])
    scale = (length_x / 2.0) ** 2
    wx2 = np.stack([np.repeat((k * k / scale)[:, None], LANES, 1) for k in wave_table(length_x)])
    every = np.concatenate(wave_table(length_y)).reshape(parts, 1, slots)
    wy2 = np.tile(every * every / scale, (1, 1, pack))
    tables = [jnp.asarray(m) for m in (fwd_y, inv_y, fwd_x, inv_x)]
    tables += [jnp.asarray(m.astype(np.float32)) for m in (wx2, wy2)]
    vmem = pl.BlockSpec(memory_space=pltpu.VMEM)
    smem = pl.BlockSpec(memory_space=pltpu.SMEM)
    anywhere = pl.BlockSpec(memory_space=pl.ANY)
    block = pltpu.VMEM((chunks, parts, 2, rows, LANES), jnp.float32)
    sems = pltpu.SemaphoreType.DMA((chunks,))
    shape = jax.ShapeDtypeStruct(heat.shape, jnp.float32)
    return pl.pallas_call(
        functools.partial(kernel, parts, levs, slots),
        out_shape=(shape, shape),
        in_specs=[vmem, vmem, anywhere, smem, smem, smem] + [vmem] * 6,
        out_specs=(vmem, vmem),
        scratch_shapes=[
            block, block, block, block,
            pltpu.VMEM((3, layers + 2, rows, length_y), jnp.float32),
            sems, sems, sems, sems,
            pltpu.SemaphoreType.DMA,
            pltpu.SemaphoreType.DMA((2, 2)),
            pltpu.SemaphoreType.DMA((2, 2)),
        ],
        compiler_params=pltpu.CompilerParams(
            collective_id=0, has_side_effects=True, vmem_limit_bytes=58 * 2**20
        ),
    )(heat, salt, speed, rate_t, rate_s, rate_c, *tables)


def solution(mesh):
    field = P("lev", "hor", None)
    in_specs = (field, field, field, P("lev"), P("lev"), P("lev"))
    return jax.shard_map(
        shards, mesh=mesh, in_specs=in_specs, out_specs=(field, field), check_vma=False
    )
```

```python
import functools
import math

import jax
import jax.numpy as jnp
import ml_dtypes
import numpy as np
from jax import lax
from jax.experimental import pallas as pl
from jax.experimental.pallas import tpu as pltpu
from jax.sharding import PartitionSpec as P

MESH = pl.DeviceIdType.MESH
LANES = 128
buoyancy = 0.5
advective_number = 0.25


def wave_table(length):
    half = length // 2
    waves = []
    for parity in range(2):
        k = np.repeat(2 * np.arange(half // 2) + parity, 2)
        if parity == 0:
            k[1] = half
        waves.append(k)
    return waves


def basis(length):
    half = length // 2
    points = np.arange(half)
    out = []
    for parity, k in enumerate(wave_table(length)):
        angle = 2.0 * math.pi / length * ((k[:, None] * points[None, :]) % length)
        rows = np.where(np.arange(half)[:, None] % 2 == 0, np.cos(angle), np.sin(angle))
        rows = rows * math.sqrt(2.0 / length)
        if parity == 0:
            rows[0] = 1.0 / math.sqrt(length)
            rows[1] = np.cos(math.pi * points) / math.sqrt(length)
        out.append(rows)
    return out


def thirds(matrix, axis):
    high = matrix.astype(ml_dtypes.bfloat16)
    low = (matrix - high.astype(np.float64)).astype(ml_dtypes.bfloat16)
    return np.concatenate([high, high, low], axis=axis)


def split3(x, axis):
    high = x.astype(jnp.bfloat16)
    low = (x - high.astype(jnp.float32)).astype(jnp.bfloat16)
    return jnp.concatenate([high, low, high], axis=axis)


def dot(a, b):
    return jnp.dot(a, b, preferred_element_type=jnp.float32)


def block_transpose(tiles, width, lane):
    count = len(tiles)
    tiles = list(tiles)
    step = count // 2
    while step >= 1:
        keep = (lane // width) % (2 * step) < step
        for i in range(count):
            if i & step == 0:
                a, b = tiles[i], tiles[i + step]
                tiles[i] = jnp.where(keep, a, pltpu.roll(b, step * width, 1))
                tiles[i + step] = jnp.where(
                    keep, pltpu.roll(a, LANES - step * width, 1), b
                )
        step //= 2
    return tiles


def kernel(
    parts, levs, slots,
    heat, salt, speed, rate_t, rate_s, rate_c, *rest
):
    sources, rest = rest[:6], rest[6:]
    filtered, speed_ends = rest[:2]
    send, recv, back_send, back_recv, field, new, *tables = rest[2:14]
    fwd_y, inv_y, fwd_x, inv_x, wx2, wy2 = tables
    send_sem, recv_sem, back_send_sem, back_recv_sem = rest[14:18]
    field_sem, new_sem, table_sem, halo_send, halo_recv = rest[18:]
    layers, rows, length_y = heat.shape
    pack = LANES // slots
    chunks = layers // pack
    half_y = length_y // 2
    length_x = rows * parts
    half_x = length_x // 2
    me = lax.axis_index("hor")
    lev = lax.axis_index("lev")
    has_low = lev > 0
    has_high = lev < levs - 1

    def peer(d):
        return lax.rem(me + d, parts)

    barrier = pltpu.get_barrier_semaphore()

    def greet(d, carry):
        pl.semaphore_signal(barrier, inc=1, device_id={"hor": peer(d)}, device_id_type=MESH)
        return carry

    lax.fori_loop(1, parts, greet, 0)

    @pl.when(has_low)
    def _():
        pl.semaphore_signal(barrier, inc=1, device_id={"lev": lev - 1}, device_id_type=MESH)

    @pl.when(has_high)
    def _():
        pl.semaphore_signal(barrier, inc=1, device_id={"lev": lev + 1}, device_id_type=MESH)

    def field_copy(f, c):
        level = pl.ds(c * pack, pack)
        return pltpu.make_async_copy(
            (heat, salt)[f].at[level], field.at[f, level], field_sem.at[f, c]
        )

    def table_copy(k):
        return pltpu.make_async_copy(sources[k], tables[k], table_sem.at[k])

    def new_copy(c):
        return pltpu.make_async_copy(
            new.at[:, pl.ds(c * pack, pack)],
            filtered.at[:, pl.ds(1 + c * pack, pack)],
            new_sem.at[c],
        )

    def chunk_of(i):
        return lax.rem(i + chunks - 1, chunks)

    def read(i, carry):
        field_copy(0, chunk_of(i)).start()
        field_copy(1, chunk_of(i)).start()
        return carry

    table_copy(0).start()
    lax.fori_loop(0, chunks, read, 0)
    for k in range(1, len(tables)):
        table_copy(k).start()

    def halo(up, kind):
        level, place = (layers - 1, 0) if up else (0, 1)
        if kind == 0:
            source, target = speed.at[level], speed_ends.at[place]
        else:
            source, target = new.at[:, level], filtered.at[:, place * (layers + 1)]
        way = 0 if up else 1
        return pltpu.make_async_remote_copy(
            src_ref=source,
            dst_ref=target,
            send_sem=halo_send.at[way, kind],
            recv_sem=halo_recv.at[way, kind],
            device_id={"lev": lev + 1 if up else lev - 1},
            device_id_type=MESH,
        )

    halo_up = functools.partial(halo, True)
    halo_down = functools.partial(halo, False)

    def send_halo(kind):
        @pl.when(has_high)
        def _():
            halo_up(kind).start()

        @pl.when(has_low)
        def _():
            halo_down(kind).start()

    def wait_halo(kind):
        @pl.when(has_high)
        def _():
            halo_up(kind).wait_send()
            halo_down(kind).wait_recv()

        @pl.when(has_low)
        def _():
            halo_down(kind).wait_send()
            halo_up(kind).wait_recv()

    def lane_of(shape):
        return lax.broadcasted_iota(jnp.int32, shape, 1)

    def exchange(source, target, s_sem, r_sem, c):
        def one(d, carry):
            q = peer(d)
            pltpu.make_async_remote_copy(
                src_ref=source.at[c, q],
                dst_ref=target.at[c, me],
                send_sem=s_sem.at[c],
                recv_sem=r_sem.at[c],
                device_id={"hor": q},
                device_id_type=MESH,
            ).start()
            return carry

        lax.fori_loop(1, parts, one, 0)
        target[c, me] = source[c, me]

    def wait_all(ref, sem, c):
        view = ref.at[c, pl.ds(0, parts - 1)]
        pltpu.make_async_copy(view, view, sem.at[c]).wait()

    def north(c):
        level = pl.ds(c * pack, pack)
        x = jnp.concatenate(
            [field[f, level].reshape(pack * rows, length_y) for f in range(2)], axis=0
        )
        a, b = x[:, :half_y], x[:, half_y:]
        spectra = [
            dot(split3(a + b, 1), fwd_y[0]).reshape(2, pack, rows, half_y),
            dot(split3(a - b, 1), fwd_y[1]).reshape(2, pack, rows, half_y),
        ]
        lane = lane_of((rows, LANES))
        for parity in range(2):
            for tile in range(half_y // LANES):
                q0 = (parity * (half_y // LANES) + tile) * pack
                cols = slice(tile * LANES, (tile + 1) * LANES)
                for f in range(2):
                    tiles = [spectra[parity][f, z, :, cols] for z in range(pack)]
                    for i, t in enumerate(block_transpose(tiles, slots, lane)):
                        send[c, q0 + i, f] = t

    def east(c):
        both = jnp.concatenate(
            [recv[c, :, f].reshape(length_x, LANES) for f in range(2)], axis=1
        )
        a, b = both[:half_x], both[half_x:]
        block = lane_of((1, LANES)) // slots
        rates = []
        for ref in (rate_t, rate_s, rate_c):
            row = jnp.full((1, LANES), ref[c * pack], jnp.float32)
            for z in range(1, pack):
                row = jnp.where(block == z, ref[c * pack + z], row)
            rates.append(row)
        waves_y = wy2[me]
        result = []
        for parity, x in enumerate((a + b, a - b)):
            spec = dot(fwd_x[parity], split3(x, 0))
            t, s = spec[:, :LANES], spec[:, LANES:]
            modulus = wx2[parity] + waves_y
            diag_t = 1.0 + rates[0] * modulus
            diag_s = 1.0 + rates[1] * modulus
            cross = rates[2] * modulus
            inverse = 1.0 / (diag_t * diag_s + cross * cross)
            new = jnp.concatenate(
                [(diag_s * t - cross * s) * inverse, (diag_t * s + cross * t) * inverse], axis=1
            )
            result.append(dot(inv_x[parity], split3(new, 0)))
        for k, x in enumerate((result[0] + result[1], result[0] - result[1])):
            for f in range(2):
                back_send[c, pl.ds(k * (parts // 2), parts // 2), f] = x[
                    :, f * LANES : (f + 1) * LANES
                ].reshape(parts // 2, rows, LANES)

    def south(c):
        lane = lane_of((rows, LANES))
        ends = []
        for parity in range(2):
            fields = []
            columns = []
            for f in range(2):
                by_tile = []
                for tile in range(half_y // LANES):
                    q0 = (parity * (half_y // LANES) + tile) * pack
                    tiles = [back_recv[c, q0 + i, f] for i in range(pack)]
                    by_tile.append(block_transpose(tiles, slots, lane))
                for z in range(pack):
                    columns.append(jnp.concatenate([t[z] for t in by_tile], axis=1))
            x = jnp.concatenate(columns, axis=0)
            ends.append(dot(split3(x, 1), inv_y[parity]))
        for k, x in enumerate((ends[0] + ends[1], ends[0] - ends[1])):
            new[:, pl.ds(c * pack, pack), :, pl.ds(k * half_y, half_y)] = x.reshape(
                2, pack, rows, half_y
            )

    def forward(i):
        c = chunk_of(i)
        field_copy(0, c).wait()
        field_copy(1, c).wait()
        north(c)
        return c

    table_copy(0).wait()
    first = forward(0)
    pl.semaphore_wait(
        barrier, parts - 1 + jnp.where(has_low, 1, 0) + jnp.where(has_high, 1, 0)
    )
    exchange(send, recv, send_sem, recv_sem, first)

    def outward(i, carry):
        exchange(send, recv, send_sem, recv_sem, forward(i))
        return carry

    lax.fori_loop(1, chunks, outward, 0)
    send_halo(0)
    for k in range(1, len(tables)):
        table_copy(k).wait()

    def middle(i, carry):
        c = chunk_of(i)
        wait_all(recv, recv_sem, c)
        east(c)
        exchange(back_send, back_recv, back_send_sem, back_recv_sem, c)
        return carry

    lax.fori_loop(0, chunks, middle, 0)

    def backward(i, carry):
        c = chunk_of(i)
        wait_all(back_recv, back_recv_sem, c)
        south(c)
        new_copy(c).start()

        @pl.when(i == 1)
        def _():
            send_halo(1)

        return carry

    lax.fori_loop(0, chunks, backward, 0)
    wait_halo(0)
    wait_halo(1)

    def drain(c, carry):
        new_copy(c).wait()
        wait_all(send, send_sem, c)
        wait_all(back_send, back_send_sem, c)
        return carry

    lax.fori_loop(0, chunks, drain, 0)


def advect(levs, filtered, speed, speed_ends, out_t, out_s):
    layers = speed.shape[0]
    lev = lax.axis_index("lev")

    def level_of(j):
        w = speed_ends[j // (layers + 1)] if j in (0, layers + 1) else speed[j - 1]
        return filtered[0, j], filtered[1, j], w

    low = level_of(0)
    below = None
    for j in range(layers + 1):
        high = level_of(j + 1)
        flow = 0.5 * (low[2] + high[2]) + buoyancy * 0.5 * (
            (low[0] + high[0]) - (low[1] + high[1])
        )
        up, down = jnp.maximum(flow, 0.0), jnp.minimum(flow, 0.0)
        above = [up * low[f] + down * high[f] for f in range(2)]
        if j == 0:
            above = [jnp.where(lev > 0, x, 0.0) for x in above]
        if j == layers:
            above = [jnp.where(lev < levs - 1, x, 0.0) for x in above]
        if j > 0:
            out_t[j - 1] = low[0] - advective_number * (above[0] - below[0])
            out_s[j - 1] = low[1] - advective_number * (above[1] - below[1])
        low, below = high, above


def shards(heat, salt, speed, rate_t, rate_s, rate_c):
    layers, rows, length_y = heat.shape
    parts = lax.axis_size("hor")
    levs = lax.axis_size("lev")
    length_x = rows * parts
    slots = length_y // parts
    pack = LANES // slots
    chunks = layers // pack
    rows_y, rows_x = basis(length_y), basis(length_x)
    fwd_y = np.stack([thirds(m.T, 0) for m in rows_y])
    inv_y = np.stack([thirds(m, 0) for m in rows_y])
    fwd_x = np.stack([thirds(m, 1) for m in rows_x])
    inv_x = np.stack([thirds(m.T, 1) for m in rows_x])
    scale = (length_x / 2.0) ** 2
    wx2 = np.stack([np.repeat((k * k / scale)[:, None], LANES, 1) for k in wave_table(length_x)])
    every = np.concatenate(wave_table(length_y)).reshape(parts, 1, slots)
    wy2 = np.tile(every * every / scale, (1, 1, pack))
    tables = [jnp.asarray(m) for m in (fwd_y, inv_y, fwd_x, inv_x)]
    tables += [jnp.asarray(m.astype(np.float32)) for m in (wx2, wy2)]
    smem = pl.BlockSpec(memory_space=pltpu.SMEM)
    anywhere = pl.BlockSpec(memory_space=pl.ANY)
    block = pltpu.VMEM((chunks, parts, 2, rows, LANES), jnp.float32)
    sems = pltpu.SemaphoreType.DMA((chunks,))
    whole = pltpu.VMEM((2, layers, rows, length_y), jnp.float32)
    filtered, speed_ends = pl.pallas_call(
        functools.partial(kernel, parts, levs, slots),
        out_shape=(
            jax.ShapeDtypeStruct((2, layers + 2, rows, length_y), jnp.float32),
            jax.ShapeDtypeStruct((2, rows, length_y), jnp.float32),
        ),
        in_specs=[anywhere] * 3 + [smem] * 3 + [anywhere] * 6,
        out_specs=(anywhere, anywhere),
        scratch_shapes=[block] * 4
        + [whole] * 2
        + [pltpu.VMEM(t.shape, t.dtype) for t in tables]
        + [sems] * 4
        + [
            pltpu.SemaphoreType.DMA((2, chunks)),
            sems,
            pltpu.SemaphoreType.DMA((len(tables),)),
            pltpu.SemaphoreType.DMA((2, 2)),
            pltpu.SemaphoreType.DMA((2, 2)),
        ],
        compiler_params=pltpu.CompilerParams(
            collective_id=0, has_side_effects=True, vmem_limit_bytes=58 * 2**20
        ),
    )(heat, salt, speed, rate_t, rate_s, rate_c, *tables)
    wide = min(length_y, 2 * LANES)
    level = pl.BlockSpec((layers, 8, wide), lambda i, k: (0, i, k))
    shape = jax.ShapeDtypeStruct(heat.shape, jnp.float32)
    return pl.pallas_call(
        functools.partial(advect, levs),
        grid=(rows // 8, length_y // wide),
        out_shape=(shape, shape),
        in_specs=[
            pl.BlockSpec((2, layers + 2, 8, wide), lambda i, k: (0, 0, i, k)),
            level,
            pl.BlockSpec((2, 8, wide), lambda i, k: (0, i, k)),
        ],
        out_specs=(level, level),
        compiler_params=pltpu.CompilerParams(vmem_limit_bytes=32 * 2**20),
    )(filtered, speed, speed_ends)


def solution(mesh):
    field = P("lev", "hor", None)
    in_specs = (field, field, field, P("lev"), P("lev"), P("lev"))
    return jax.shard_map(
        shards, mesh=mesh, in_specs=in_specs, out_specs=(field, field), check_vma=False
    )
```

```python
import functools
import math

import jax
import jax.numpy as jnp
import ml_dtypes
import numpy as np
from jax import lax
from jax.experimental import pallas as pl
from jax.experimental.pallas import tpu as pltpu
from jax.sharding import PartitionSpec as P

MESH = pl.DeviceIdType.MESH
LANES = 128
buoyancy = 0.5
advective_number = 0.25


def wave_table(length):
    half = length // 2
    waves = []
    for parity in range(2):
        k = np.repeat(2 * np.arange(half // 2) + parity, 2)
        if parity == 0:
            k[1] = half
        waves.append(k)
    return waves


def basis(length):
    half = length // 2
    points = np.arange(half)
    out = []
    for parity, k in enumerate(wave_table(length)):
        angle = 2.0 * math.pi / length * ((k[:, None] * points[None, :]) % length)
        rows = np.where(np.arange(half)[:, None] % 2 == 0, np.cos(angle), np.sin(angle))
        rows = rows * math.sqrt(2.0 / length)
        if parity == 0:
            rows[0] = 1.0 / math.sqrt(length)
            rows[1] = np.cos(math.pi * points) / math.sqrt(length)
        out.append(rows)
    return out


def thirds(matrix, axis):
    high = matrix.astype(ml_dtypes.bfloat16)
    low = (matrix - high.astype(np.float64)).astype(ml_dtypes.bfloat16)
    return np.concatenate([high, high, low], axis=axis)


def split3(x, axis):
    high = x.astype(jnp.bfloat16)
    low = (x - high.astype(jnp.float32)).astype(jnp.bfloat16)
    return jnp.concatenate([high, low, high], axis=axis)


def dot(a, b):
    return jnp.dot(a, b, preferred_element_type=jnp.float32)


def block_transpose(tiles, width, lane):
    count = len(tiles)
    tiles = list(tiles)
    step = count // 2
    while step >= 1:
        keep = (lane // width) % (2 * step) < step
        for i in range(count):
            if i & step == 0:
                a, b = tiles[i], tiles[i + step]
                tiles[i] = jnp.where(keep, a, pltpu.roll(b, step * width, 1))
                tiles[i + step] = jnp.where(
                    keep, pltpu.roll(a, LANES - step * width, 1), b
                )
        step //= 2
    return tiles


def kernel(
    parts, levs, slots,
    heat, salt, speed, rate_t, rate_s, rate_c, *rest
):
    sources, rest = rest[:6], rest[6:]
    filtered, speed_ends = rest[:2]
    send, recv, back_send, back_recv, field, new, *tables = rest[2:14]
    fwd_y, inv_y, fwd_x, inv_x, wx2, wy2 = tables
    send_sem, recv_sem, back_send_sem, back_recv_sem = rest[14:18]
    field_sem, new_sem, table_sem, halo_send, halo_recv = rest[18:]
    layers, rows, length_y = heat.shape
    pack = LANES // slots
    chunks = layers // pack
    half_y = length_y // 2
    length_x = rows * parts
    half_x = length_x // 2
    me = lax.axis_index("hor")
    lev = lax.axis_index("lev")
    has_low = lev > 0
    has_high = lev < levs - 1

    def peer(d):
        return lax.rem(me + d, parts)

    barrier = pltpu.get_barrier_semaphore()

    def greet(d, carry):
        pl.semaphore_signal(barrier, inc=1, device_id={"hor": peer(d)}, device_id_type=MESH)
        return carry

    lax.fori_loop(1, parts, greet, 0)

    @pl.when(has_low)
    def _():
        pl.semaphore_signal(barrier, inc=1, device_id={"lev": lev - 1}, device_id_type=MESH)

    @pl.when(has_high)
    def _():
        pl.semaphore_signal(barrier, inc=1, device_id={"lev": lev + 1}, device_id_type=MESH)

    def field_copy(f, c):
        level = pl.ds(c * pack, pack)
        return pltpu.make_async_copy(
            (heat, salt)[f].at[level], field.at[f, level], field_sem.at[f, c]
        )

    def table_copy(k):
        return pltpu.make_async_copy(sources[k], tables[k], table_sem.at[k])

    def new_copy(c):
        return pltpu.make_async_copy(
            new.at[:, pl.ds(c * pack, pack)],
            filtered.at[:, pl.ds(1 + c * pack, pack)],
            new_sem.at[c],
        )

    def chunk_of(i):
        return lax.rem(i + chunks - 1, chunks)

    def read(i, carry):
        field_copy(0, chunk_of(i)).start()
        field_copy(1, chunk_of(i)).start()
        return carry

    table_copy(0).start()
    lax.fori_loop(0, chunks, read, 0)
    for k in range(1, len(tables)):
        table_copy(k).start()

    def halo(up, kind):
        level, place = (layers - 1, 0) if up else (0, 1)
        if kind == 0:
            source, target = speed.at[level], speed_ends.at[place]
        else:
            source, target = new.at[:, level], filtered.at[:, place * (layers + 1)]
        way = 0 if up else 1
        return pltpu.make_async_remote_copy(
            src_ref=source,
            dst_ref=target,
            send_sem=halo_send.at[way, kind],
            recv_sem=halo_recv.at[way, kind],
            device_id={"lev": lev + 1 if up else lev - 1},
            device_id_type=MESH,
        )

    halo_up = functools.partial(halo, True)
    halo_down = functools.partial(halo, False)

    def send_halo(kind):
        @pl.when(has_high)
        def _():
            halo_up(kind).start()

        @pl.when(has_low)
        def _():
            halo_down(kind).start()

    def wait_halo(kind):
        @pl.when(has_high)
        def _():
            halo_up(kind).wait_send()
            halo_down(kind).wait_recv()

        @pl.when(has_low)
        def _():
            halo_down(kind).wait_send()
            halo_up(kind).wait_recv()

    def lane_of(shape):
        return lax.broadcasted_iota(jnp.int32, shape, 1)

    stride = max(1, parts // 4)
    while math.gcd(stride, parts - 1) > 1:
        stride += 1

    def exchange(source, target, s_sem, r_sem, c):
        def one(i, carry):
            q = peer(1 + lax.rem(i * stride + me, parts - 1))
            pltpu.make_async_remote_copy(
                src_ref=source.at[c, q],
                dst_ref=target.at[c, me],
                send_sem=s_sem.at[c],
                recv_sem=r_sem.at[c],
                device_id={"hor": q},
                device_id_type=MESH,
            ).start()
            return carry

        lax.fori_loop(1, parts, one, 0)
        target[c, me] = source[c, me]

    def wait_all(ref, sem, c):
        view = ref.at[c, pl.ds(0, parts - 1)]
        pltpu.make_async_copy(view, view, sem.at[c]).wait()

    def north(c):
        level = pl.ds(c * pack, pack)
        x = jnp.concatenate(
            [field[f, level].reshape(pack * rows, length_y) for f in range(2)], axis=0
        )
        a, b = x[:, :half_y], x[:, half_y:]
        spectra = [
            dot(split3(a + b, 1), fwd_y[0]).reshape(2, pack, rows, half_y),
            dot(split3(a - b, 1), fwd_y[1]).reshape(2, pack, rows, half_y),
        ]
        lane = lane_of((rows, LANES))
        for parity in range(2):
            for tile in range(half_y // LANES):
                q0 = (parity * (half_y // LANES) + tile) * pack
                cols = slice(tile * LANES, (tile + 1) * LANES)
                for f in range(2):
                    tiles = [spectra[parity][f, z, :, cols] for z in range(pack)]
                    for i, t in enumerate(block_transpose(tiles, slots, lane)):
                        send[c, q0 + i, f] = t

    def east(c):
        both = jnp.concatenate(
            [recv[c, :, f].reshape(length_x, LANES) for f in range(2)], axis=1
        )
        a, b = both[:half_x], both[half_x:]
        block = lane_of((1, LANES)) // slots
        rates = []
        for ref in (rate_t, rate_s, rate_c):
            row = jnp.full((1, LANES), ref[c * pack], jnp.float32)
            for z in range(1, pack):
                row = jnp.where(block == z, ref[c * pack + z], row)
            rates.append(row)
        waves_y = wy2[me]
        result = []
        for parity, x in enumerate((a + b, a - b)):
            spec = dot(fwd_x[parity], split3(x, 0))
            t, s = spec[:, :LANES], spec[:, LANES:]
            modulus = wx2[parity] + waves_y
            diag_t = 1.0 + rates[0] * modulus
            diag_s = 1.0 + rates[1] * modulus
            cross = rates[2] * modulus
            inverse = 1.0 / (diag_t * diag_s + cross * cross)
            new = jnp.concatenate(
                [(diag_s * t - cross * s) * inverse, (diag_t * s + cross * t) * inverse], axis=1
            )
            result.append(dot(inv_x[parity], split3(new, 0)))
        for k, x in enumerate((result[0] + result[1], result[0] - result[1])):
            for f in range(2):
                back_send[c, pl.ds(k * (parts // 2), parts // 2), f] = x[
                    :, f * LANES : (f + 1) * LANES
                ].reshape(parts // 2, rows, LANES)

    def south(c):
        lane = lane_of((rows, LANES))
        ends = []
        for parity in range(2):
            fields = []
            columns = []
            for f in range(2):
                by_tile = []
                for tile in range(half_y // LANES):
                    q0 = (parity * (half_y // LANES) + tile) * pack
                    tiles = [back_recv[c, q0 + i, f] for i in range(pack)]
                    by_tile.append(block_transpose(tiles, slots, lane))
                for z in range(pack):
                    columns.append(jnp.concatenate([t[z] for t in by_tile], axis=1))
            x = jnp.concatenate(columns, axis=0)
            ends.append(dot(split3(x, 1), inv_y[parity]))
        for k, x in enumerate((ends[0] + ends[1], ends[0] - ends[1])):
            new[:, pl.ds(c * pack, pack), :, pl.ds(k * half_y, half_y)] = x.reshape(
                2, pack, rows, half_y
            )

    def forward(i):
        c = chunk_of(i)
        field_copy(0, c).wait()
        field_copy(1, c).wait()
        north(c)
        return c

    table_copy(0).wait()
    first = forward(0)
    pl.semaphore_wait(
        barrier, parts - 1 + jnp.where(has_low, 1, 0) + jnp.where(has_high, 1, 0)
    )
    exchange(send, recv, send_sem, recv_sem, first)

    def outward(i, carry):
        exchange(send, recv, send_sem, recv_sem, forward(i))
        return carry

    lax.fori_loop(1, chunks, outward, 0)
    send_halo(0)
    for k in range(1, len(tables)):
        table_copy(k).wait()

    def middle(i, carry):
        c = chunk_of(i)
        wait_all(recv, recv_sem, c)
        east(c)
        exchange(back_send, back_recv, back_send_sem, back_recv_sem, c)
        return carry

    lax.fori_loop(0, chunks, middle, 0)

    def backward(i, carry):
        c = chunk_of(i)
        wait_all(back_recv, back_recv_sem, c)
        south(c)
        new_copy(c).start()

        @pl.when(i == 1)
        def _():
            send_halo(1)

        return carry

    lax.fori_loop(0, chunks, backward, 0)
    wait_halo(0)
    wait_halo(1)

    def drain(c, carry):
        new_copy(c).wait()
        wait_all(send, send_sem, c)
        wait_all(back_send, back_send_sem, c)
        return carry

    lax.fori_loop(0, chunks, drain, 0)


def advect(levs, filtered, speed, speed_ends, out_t, out_s):
    layers = speed.shape[0]
    lev = lax.axis_index("lev")

    def level_of(j):
        w = speed_ends[j // (layers + 1)] if j in (0, layers + 1) else speed[j - 1]
        return filtered[0, j], filtered[1, j], w

    low = level_of(0)
    below = None
    for j in range(layers + 1):
        high = level_of(j + 1)
        flow = 0.5 * (low[2] + high[2]) + buoyancy * 0.5 * (
            (low[0] + high[0]) - (low[1] + high[1])
        )
        up, down = jnp.maximum(flow, 0.0), jnp.minimum(flow, 0.0)
        above = [up * low[f] + down * high[f] for f in range(2)]
        if j == 0:
            above = [jnp.where(lev > 0, x, 0.0) for x in above]
        if j == layers:
            above = [jnp.where(lev < levs - 1, x, 0.0) for x in above]
        if j > 0:
            out_t[j - 1] = low[0] - advective_number * (above[0] - below[0])
            out_s[j - 1] = low[1] - advective_number * (above[1] - below[1])
        low, below = high, above


def shards(heat, salt, speed, rate_t, rate_s, rate_c):
    layers, rows, length_y = heat.shape
    parts = lax.axis_size("hor")
    levs = lax.axis_size("lev")
    length_x = rows * parts
    slots = length_y // parts
    pack = LANES // slots
    chunks = layers // pack
    rows_y, rows_x = basis(length_y), basis(length_x)
    fwd_y = np.stack([thirds(m.T, 0) for m in rows_y])
    inv_y = np.stack([thirds(m, 0) for m in rows_y])
    fwd_x = np.stack([thirds(m, 1) for m in rows_x])
    inv_x = np.stack([thirds(m.T, 1) for m in rows_x])
    scale = (length_x / 2.0) ** 2
    wx2 = np.stack([np.repeat((k * k / scale)[:, None], LANES, 1) for k in wave_table(length_x)])
    every = np.concatenate(wave_table(length_y)).reshape(parts, 1, slots)
    wy2 = np.tile(every * every / scale, (1, 1, pack))
    tables = [jnp.asarray(m) for m in (fwd_y, inv_y, fwd_x, inv_x)]
    tables += [jnp.asarray(m.astype(np.float32)) for m in (wx2, wy2)]
    smem = pl.BlockSpec(memory_space=pltpu.SMEM)
    anywhere = pl.BlockSpec(memory_space=pl.ANY)
    block = pltpu.VMEM((chunks, parts, 2, rows, LANES), jnp.float32)
    sems = pltpu.SemaphoreType.DMA((chunks,))
    whole = pltpu.VMEM((2, layers, rows, length_y), jnp.float32)
    filtered, speed_ends = pl.pallas_call(
        functools.partial(kernel, parts, levs, slots),
        out_shape=(
            jax.ShapeDtypeStruct((2, layers + 2, rows, length_y), jnp.float32),
            jax.ShapeDtypeStruct((2, rows, length_y), jnp.float32),
        ),
        in_specs=[anywhere] * 3 + [smem] * 3 + [anywhere] * 6,
        out_specs=(anywhere, anywhere),
        scratch_shapes=[block] * 4
        + [whole] * 2
        + [pltpu.VMEM(t.shape, t.dtype) for t in tables]
        + [sems] * 4
        + [
            pltpu.SemaphoreType.DMA((2, chunks)),
            sems,
            pltpu.SemaphoreType.DMA((len(tables),)),
            pltpu.SemaphoreType.DMA((2, 2)),
            pltpu.SemaphoreType.DMA((2, 2)),
        ],
        compiler_params=pltpu.CompilerParams(
            collective_id=0, has_side_effects=True, vmem_limit_bytes=58 * 2**20
        ),
    )(heat, salt, speed, rate_t, rate_s, rate_c, *tables)
    wide = min(length_y, 2 * LANES)
    level = pl.BlockSpec((layers, 8, wide), lambda i, k: (0, i, k))
    shape = jax.ShapeDtypeStruct(heat.shape, jnp.float32)
    return pl.pallas_call(
        functools.partial(advect, levs),
        grid=(rows // 8, length_y // wide),
        out_shape=(shape, shape),
        in_specs=[
            pl.BlockSpec((2, layers + 2, 8, wide), lambda i, k: (0, 0, i, k)),
            level,
            pl.BlockSpec((2, 8, wide), lambda i, k: (0, i, k)),
        ],
        out_specs=(level, level),
        compiler_params=pltpu.CompilerParams(vmem_limit_bytes=58 * 2**20),
    )(filtered, speed, speed_ends)


def solution(mesh):
    field = P("lev", "hor", None)
    in_specs = (field, field, field, P("lev"), P("lev"), P("lev"))
    return jax.shard_map(
        shards, mesh=mesh, in_specs=in_specs, out_specs=(field, field), check_vma=False
    )
```

```python
import functools
import math

import jax
import jax.numpy as jnp
import ml_dtypes
import numpy as np
from jax import lax
from jax.experimental import pallas as pl
from jax.experimental.pallas import tpu as pltpu
from jax.sharding import PartitionSpec as P

MESH = pl.DeviceIdType.MESH
LANES = 128
buoyancy = 0.5
advective_number = 0.25


def wave_table(length):
    half = length // 2
    waves = []
    for parity in range(2):
        k = np.repeat(2 * np.arange(half // 2) + parity, 2)
        if parity == 0:
            k[1] = half
        waves.append(k)
    return waves


def basis(length):
    half = length // 2
    points = np.arange(half)
    out = []
    for parity, k in enumerate(wave_table(length)):
        angle = 2.0 * math.pi / length * ((k[:, None] * points[None, :]) % length)
        rows = np.where(np.arange(half)[:, None] % 2 == 0, np.cos(angle), np.sin(angle))
        rows = rows * math.sqrt(2.0 / length)
        if parity == 0:
            rows[0] = 1.0 / math.sqrt(length)
            rows[1] = np.cos(math.pi * points) / math.sqrt(length)
        out.append(rows)
    return out


def thirds(matrix, axis):
    high = matrix.astype(ml_dtypes.bfloat16)
    low = (matrix - high.astype(np.float64)).astype(ml_dtypes.bfloat16)
    return np.concatenate([high, high, low], axis=axis)


def split3(x, axis):
    high = x.astype(jnp.bfloat16)
    low = (x - high.astype(jnp.float32)).astype(jnp.bfloat16)
    return jnp.concatenate([high, low, high], axis=axis)


def dot(a, b):
    return jnp.dot(a, b, preferred_element_type=jnp.float32)


def block_transpose(tiles, width, lane):
    count = len(tiles)
    tiles = list(tiles)
    step = count // 2
    while step >= 1:
        keep = (lane // width) % (2 * step) < step
        for i in range(count):
            if i & step == 0:
                a, b = tiles[i], tiles[i + step]
                tiles[i] = jnp.where(keep, a, pltpu.roll(b, step * width, 1))
                tiles[i + step] = jnp.where(
                    keep, pltpu.roll(a, LANES - step * width, 1), b
                )
        step //= 2
    return tiles


def kernel(
    parts, levs, slots,
    heat, salt, speed, rate_t, rate_s, rate_c, *rest
):
    sources, rest = rest[:6], rest[6:]
    filtered, speed_ends = rest[:2]
    send, recv, back_send, back_recv, field, new, *tables = rest[2:14]
    fwd_y, inv_y, fwd_x, inv_x, wx2, wy2 = tables
    send_sem, recv_sem, back_send_sem, back_recv_sem = rest[14:18]
    field_sem, new_sem, table_sem, halo_send, halo_recv = rest[18:]
    layers, rows, length_y = heat.shape
    pack = LANES // slots
    chunks = layers // pack
    half_y = length_y // 2
    length_x = rows * parts
    half_x = length_x // 2
    me = lax.axis_index("hor")
    lev = lax.axis_index("lev")
    has_low = lev > 0
    has_high = lev < levs - 1

    def peer(d):
        return lax.rem(me + d, parts)

    barrier = pltpu.get_barrier_semaphore()

    def greet(d, carry):
        pl.semaphore_signal(barrier, inc=1, device_id={"hor": peer(d)}, device_id_type=MESH)
        return carry

    lax.fori_loop(1, parts, greet, 0)

    @pl.when(has_low)
    def _():
        pl.semaphore_signal(barrier, inc=1, device_id={"lev": lev - 1}, device_id_type=MESH)

    @pl.when(has_high)
    def _():
        pl.semaphore_signal(barrier, inc=1, device_id={"lev": lev + 1}, device_id_type=MESH)

    def field_copy(f, c):
        level = pl.ds(c * pack, pack)
        return pltpu.make_async_copy(
            (heat, salt)[f].at[level], field.at[f, level], field_sem.at[f, c]
        )

    def table_copy(k):
        return pltpu.make_async_copy(sources[k], tables[k], table_sem.at[k])

    def new_copy(c):
        return pltpu.make_async_copy(
            new.at[:, pl.ds(c * pack, pack)],
            filtered.at[:, pl.ds(1 + c * pack, pack)],
            new_sem.at[c],
        )

    def chunk_of(i):
        return lax.rem(i + chunks - 1, chunks)

    def read(i, carry):
        field_copy(0, chunk_of(i)).start()
        field_copy(1, chunk_of(i)).start()
        return carry

    table_copy(0).start()
    lax.fori_loop(0, chunks, read, 0)
    for k in range(1, len(tables)):
        table_copy(k).start()

    def halo(up, kind):
        level, place = (layers - 1, 0) if up else (0, 1)
        if kind == 0:
            source, target = speed.at[level], speed_ends.at[place]
        else:
            source, target = new.at[:, level], filtered.at[:, place * (layers + 1)]
        way = 0 if up else 1
        return pltpu.make_async_remote_copy(
            src_ref=source,
            dst_ref=target,
            send_sem=halo_send.at[way, kind],
            recv_sem=halo_recv.at[way, kind],
            device_id={"lev": lev + 1 if up else lev - 1},
            device_id_type=MESH,
        )

    halo_up = functools.partial(halo, True)
    halo_down = functools.partial(halo, False)

    def send_halo(kind):
        @pl.when(has_high)
        def _():
            halo_up(kind).start()

        @pl.when(has_low)
        def _():
            halo_down(kind).start()

    def wait_halo(kind):
        @pl.when(has_high)
        def _():
            halo_up(kind).wait_send()
            halo_down(kind).wait_recv()

        @pl.when(has_low)
        def _():
            halo_down(kind).wait_send()
            halo_up(kind).wait_recv()

    def lane_of(shape):
        return lax.broadcasted_iota(jnp.int32, shape, 1)

    def exchange(source, target, s_sem, r_sem, c):
        def one(d, carry):
            q = peer(d)
            pltpu.make_async_remote_copy(
                src_ref=source.at[c, q],
                dst_ref=target.at[c, me],
                send_sem=s_sem.at[c],
                recv_sem=r_sem.at[c],
                device_id={"hor": q},
                device_id_type=MESH,
            ).start()
            return carry

        lax.fori_loop(1, parts, one, 0)
        target[c, me] = source[c, me]

    def wait_all(ref, sem, c):
        view = ref.at[c, pl.ds(0, parts - 1)]
        pltpu.make_async_copy(view, view, sem.at[c]).wait()

    def north(c):
        level = pl.ds(c * pack, pack)
        x = jnp.concatenate(
            [field[f, level].reshape(pack * rows, length_y) for f in range(2)], axis=0
        )
        a, b = x[:, :half_y], x[:, half_y:]
        spectra = [
            dot(split3(a + b, 1), fwd_y[0]).reshape(2, pack, rows, half_y),
            dot(split3(a - b, 1), fwd_y[1]).reshape(2, pack, rows, half_y),
        ]
        lane = lane_of((rows, LANES))
        for parity in range(2):
            for tile in range(half_y // LANES):
                q0 = (parity * (half_y // LANES) + tile) * pack
                cols = slice(tile * LANES, (tile + 1) * LANES)
                for f in range(2):
                    tiles = [spectra[parity][f, z, :, cols] for z in range(pack)]
                    for i, t in enumerate(block_transpose(tiles, slots, lane)):
                        send[c, q0 + i, f] = t

    def east(c):
        both = jnp.concatenate(
            [recv[c, :, f].reshape(length_x, LANES) for f in range(2)], axis=1
        )
        a, b = both[:half_x], both[half_x:]
        block = lane_of((1, LANES)) // slots
        rates = []
        for ref in (rate_t, rate_s, rate_c):
            row = jnp.full((1, LANES), ref[c * pack], jnp.float32)
            for z in range(1, pack):
                row = jnp.where(block == z, ref[c * pack + z], row)
            rates.append(row)
        waves_y = wy2[me]
        result = []
        for parity, x in enumerate((a + b, a - b)):
            spec = dot(fwd_x[parity], split3(x, 0))
            t, s = spec[:, :LANES], spec[:, LANES:]
            modulus = wx2[parity] + waves_y
            diag_t = 1.0 + rates[0] * modulus
            diag_s = 1.0 + rates[1] * modulus
            cross = rates[2] * modulus
            inverse = 1.0 / (diag_t * diag_s + cross * cross)
            new = jnp.concatenate(
                [(diag_s * t - cross * s) * inverse, (diag_t * s + cross * t) * inverse], axis=1
            )
            result.append(dot(inv_x[parity], split3(new, 0)))
        for k, x in enumerate((result[0] + result[1], result[0] - result[1])):
            for f in range(2):
                back_send[c, pl.ds(k * (parts // 2), parts // 2), f] = x[
                    :, f * LANES : (f + 1) * LANES
                ].reshape(parts // 2, rows, LANES)

    def south(c):
        lane = lane_of((rows, LANES))
        ends = []
        for parity in range(2):
            fields = []
            columns = []
            for f in range(2):
                by_tile = []
                for tile in range(half_y // LANES):
                    q0 = (parity * (half_y // LANES) + tile) * pack
                    tiles = [back_recv[c, q0 + i, f] for i in range(pack)]
                    by_tile.append(block_transpose(tiles, slots, lane))
                for z in range(pack):
                    columns.append(jnp.concatenate([t[z] for t in by_tile], axis=1))
            x = jnp.concatenate(columns, axis=0)
            ends.append(dot(split3(x, 1), inv_y[parity]))
        for k, x in enumerate((ends[0] + ends[1], ends[0] - ends[1])):
            new[:, pl.ds(c * pack, pack), :, pl.ds(k * half_y, half_y)] = x.reshape(
                2, pack, rows, half_y
            )

    def forward(i):
        c = chunk_of(i)
        field_copy(0, c).wait()
        field_copy(1, c).wait()
        north(c)
        return c

    table_copy(0).wait()
    first = forward(0)
    pl.semaphore_wait(
        barrier, parts - 1 + jnp.where(has_low, 1, 0) + jnp.where(has_high, 1, 0)
    )
    exchange(send, recv, send_sem, recv_sem, first)

    def outward(i, carry):
        exchange(send, recv, send_sem, recv_sem, forward(i))
        return carry

    lax.fori_loop(1, chunks, outward, 0)
    send_halo(0)
    for k in range(1, len(tables)):
        table_copy(k).wait()

    def middle(i, carry):
        c = chunk_of(i)
        wait_all(recv, recv_sem, c)
        east(c)
        exchange(back_send, back_recv, back_send_sem, back_recv_sem, c)
        return carry

    lax.fori_loop(0, chunks, middle, 0)

    def backward(i, carry):
        c = chunk_of(i)
        wait_all(back_recv, back_recv_sem, c)
        south(c)
        new_copy(c).start()

        @pl.when(i == 1)
        def _():
            send_halo(1)

        return carry

    lax.fori_loop(0, chunks, backward, 0)
    wait_halo(0)
    wait_halo(1)

    def drain(c, carry):
        new_copy(c).wait()
        wait_all(send, send_sem, c)
        wait_all(back_send, back_send_sem, c)
        return carry

    lax.fori_loop(0, chunks, drain, 0)


def advect(levs, filtered, speed, speed_ends, out_t, out_s):
    layers = speed.shape[0]
    lev = lax.axis_index("lev")
    r = pl.ds(pl.multiple_of(pl.program_id(0) * 8, 8), 8)

    def level_of(j):
        w = speed_ends[j // (layers + 1), r] if j in (0, layers + 1) else speed[j - 1, r]
        return filtered[0, j, r], filtered[1, j, r], w

    low = level_of(0)
    below = None
    for j in range(layers + 1):
        high = level_of(j + 1)
        flow = 0.5 * (low[2] + high[2]) + buoyancy * 0.5 * (
            (low[0] + high[0]) - (low[1] + high[1])
        )
        up, down = jnp.maximum(flow, 0.0), jnp.minimum(flow, 0.0)
        above = [up * low[f] + down * high[f] for f in range(2)]
        if j == 0:
            above = [jnp.where(lev > 0, x, 0.0) for x in above]
        if j == layers:
            above = [jnp.where(lev < levs - 1, x, 0.0) for x in above]
        if j > 0:
            out_t[j - 1] = low[0] - advective_number * (above[0] - below[0])
            out_s[j - 1] = low[1] - advective_number * (above[1] - below[1])
        low, below = high, above


def shards(heat, salt, speed, rate_t, rate_s, rate_c):
    layers, rows, length_y = heat.shape
    parts = lax.axis_size("hor")
    levs = lax.axis_size("lev")
    length_x = rows * parts
    slots = length_y // parts
    pack = LANES // slots
    chunks = layers // pack
    rows_y, rows_x = basis(length_y), basis(length_x)
    fwd_y = np.stack([thirds(m.T, 0) for m in rows_y])
    inv_y = np.stack([thirds(m, 0) for m in rows_y])
    fwd_x = np.stack([thirds(m, 1) for m in rows_x])
    inv_x = np.stack([thirds(m.T, 1) for m in rows_x])
    scale = (length_x / 2.0) ** 2
    wx2 = np.stack([np.repeat((k * k / scale)[:, None], LANES, 1) for k in wave_table(length_x)])
    every = np.concatenate(wave_table(length_y)).reshape(parts, 1, slots)
    wy2 = np.tile(every * every / scale, (1, 1, pack))
    tables = [jnp.asarray(m) for m in (fwd_y, inv_y, fwd_x, inv_x)]
    tables += [jnp.asarray(m.astype(np.float32)) for m in (wx2, wy2)]
    smem = pl.BlockSpec(memory_space=pltpu.SMEM)
    anywhere = pl.BlockSpec(memory_space=pl.ANY)
    block = pltpu.VMEM((chunks, parts, 2, rows, LANES), jnp.float32)
    sems = pltpu.SemaphoreType.DMA((chunks,))
    whole = pltpu.VMEM((2, layers, rows, length_y), jnp.float32)
    filtered, speed_ends = pl.pallas_call(
        functools.partial(kernel, parts, levs, slots),
        out_shape=(
            pltpu.VMEM((2, layers + 2, rows, length_y), jnp.float32),
            pltpu.VMEM((2, rows, length_y), jnp.float32),
        ),
        in_specs=[anywhere] * 3 + [smem] * 3 + [anywhere] * 6,
        out_specs=(anywhere, anywhere),
        scratch_shapes=[block] * 4
        + [whole] * 2
        + [pltpu.VMEM(t.shape, t.dtype) for t in tables]
        + [sems] * 4
        + [
            pltpu.SemaphoreType.DMA((2, chunks)),
            sems,
            pltpu.SemaphoreType.DMA((len(tables),)),
            pltpu.SemaphoreType.DMA((2, 2)),
            pltpu.SemaphoreType.DMA((2, 2)),
        ],
        compiler_params=pltpu.CompilerParams(
            collective_id=0, has_side_effects=True, vmem_limit_bytes=57 * 2**20
        ),
    )(heat, salt, speed, rate_t, rate_s, rate_c, *tables)
    level = pl.BlockSpec((layers, 8, length_y), lambda i: (0, i, 0))
    whole = pl.BlockSpec(memory_space=pltpu.VMEM)
    shape = jax.ShapeDtypeStruct(heat.shape, jnp.float32)
    return pl.pallas_call(
        functools.partial(advect, levs),
        grid=(rows // 8,),
        out_shape=(shape, shape),
        in_specs=[whole] * 3,
        out_specs=(level, level),
        compiler_params=pltpu.CompilerParams(vmem_limit_bytes=16 * 2**20),
    )(filtered, speed, speed_ends)


def solution(mesh):
    field = P("lev", "hor", None)
    in_specs = (field, field, field, P("lev"), P("lev"), P("lev"))
    return jax.shard_map(
        shards, mesh=mesh, in_specs=in_specs, out_specs=(field, field), check_vma=False
    )
```

```python
import functools
import math

import jax
import jax.numpy as jnp
import ml_dtypes
import numpy as np
from jax import lax
from jax.experimental import pallas as pl
from jax.experimental.pallas import tpu as pltpu
from jax.sharding import PartitionSpec as P

MESH = pl.DeviceIdType.MESH
LANES = 128
buoyancy = 0.5
advective_number = 0.25


def wave_table(length):
    half = length // 2
    waves = []
    for parity in range(2):
        k = np.repeat(2 * np.arange(half // 2) + parity, 2)
        if parity == 0:
            k[1] = half
        waves.append(k)
    return waves


def basis(length):
    half = length // 2
    points = np.arange(half)
    out = []
    for parity, k in enumerate(wave_table(length)):
        angle = 2.0 * math.pi / length * ((k[:, None] * points[None, :]) % length)
        rows = np.where(np.arange(half)[:, None] % 2 == 0, np.cos(angle), np.sin(angle))
        rows = rows * math.sqrt(2.0 / length)
        if parity == 0:
            rows[0] = 1.0 / math.sqrt(length)
            rows[1] = np.cos(math.pi * points) / math.sqrt(length)
        out.append(rows)
    return out


def thirds(matrix, axis):
    high = matrix.astype(ml_dtypes.bfloat16)
    low = (matrix - high.astype(np.float64)).astype(ml_dtypes.bfloat16)
    return np.concatenate([high, high, low], axis=axis)


def split3(x, axis):
    high = x.astype(jnp.bfloat16)
    low = (x - high.astype(jnp.float32)).astype(jnp.bfloat16)
    return jnp.concatenate([high, low, high], axis=axis)


def dot(a, b):
    return jnp.dot(a, b, preferred_element_type=jnp.float32)


def block_transpose(tiles, width, lane):
    count = len(tiles)
    tiles = list(tiles)
    step = count // 2
    while step >= 1:
        keep = (lane // width) % (2 * step) < step
        for i in range(count):
            if i & step == 0:
                a, b = tiles[i], tiles[i + step]
                tiles[i] = jnp.where(keep, a, pltpu.roll(b, step * width, 1))
                tiles[i + step] = jnp.where(
                    keep, pltpu.roll(a, LANES - step * width, 1), b
                )
        step //= 2
    return tiles


def kernel(
    parts, levs, slots,
    heat, salt, speed, rate_t, rate_s, rate_c, *rest
):
    sources, rest = rest[:6], rest[6:]
    filtered, speed_ends = rest[:2]
    send, recv, back_send, back_recv, field, new, *tables = rest[2:14]
    fwd_y, inv_y, fwd_x, inv_x, wx2, wy2 = tables
    send_sem, recv_sem, back_send_sem, back_recv_sem = rest[14:18]
    field_sem, new_sem, table_sem, halo_send, halo_recv = rest[18:]
    layers, rows, length_y = heat.shape
    pack = LANES // slots
    chunks = layers // pack
    half_y = length_y // 2
    length_x = rows * parts
    half_x = length_x // 2
    me = lax.axis_index("hor")
    lev = lax.axis_index("lev")
    has_low = lev > 0
    has_high = lev < levs - 1

    def peer(d):
        return lax.rem(me + d, parts)

    barrier = pltpu.get_barrier_semaphore()

    def greet(d, carry):
        pl.semaphore_signal(barrier, inc=1, device_id={"hor": peer(d)}, device_id_type=MESH)
        return carry

    lax.fori_loop(1, parts, greet, 0)

    @pl.when(has_low)
    def _():
        pl.semaphore_signal(barrier, inc=1, device_id={"lev": lev - 1}, device_id_type=MESH)

    @pl.when(has_high)
    def _():
        pl.semaphore_signal(barrier, inc=1, device_id={"lev": lev + 1}, device_id_type=MESH)

    def field_copy(f, c):
        level = pl.ds(c * pack, pack)
        return pltpu.make_async_copy(
            (heat, salt)[f].at[level], field.at[f, level], field_sem.at[f, c]
        )

    def table_copy(k):
        return pltpu.make_async_copy(sources[k], tables[k], table_sem.at[k])

    def new_copy(c):
        return pltpu.make_async_copy(
            new.at[:, pl.ds(c * pack, pack)],
            filtered.at[:, pl.ds(1 + c * pack, pack)],
            new_sem.at[c],
        )

    def chunk_of(i):
        return lax.rem(i + chunks - 1, chunks)

    def read(i, carry):
        field_copy(0, chunk_of(i)).start()
        field_copy(1, chunk_of(i)).start()
        return carry

    table_copy(0).start()
    lax.fori_loop(0, chunks, read, 0)
    for k in range(1, len(tables)):
        table_copy(k).start()

    def halo(up, kind):
        level, place = (layers - 1, 0) if up else (0, 1)
        if kind == 0:
            source, target = speed.at[level], speed_ends.at[place]
        else:
            source, target = new.at[:, level], filtered.at[:, place * (layers + 1)]
        way = 0 if up else 1
        return pltpu.make_async_remote_copy(
            src_ref=source,
            dst_ref=target,
            send_sem=halo_send.at[way, kind],
            recv_sem=halo_recv.at[way, kind],
            device_id={"lev": lev + 1 if up else lev - 1},
            device_id_type=MESH,
        )

    halo_up = functools.partial(halo, True)
    halo_down = functools.partial(halo, False)

    def send_halo(kind):
        @pl.when(has_high)
        def _():
            halo_up(kind).start()

        @pl.when(has_low)
        def _():
            halo_down(kind).start()

    def wait_halo(kind):
        @pl.when(has_high)
        def _():
            halo_up(kind).wait_send()
            halo_down(kind).wait_recv()

        @pl.when(has_low)
        def _():
            halo_down(kind).wait_send()
            halo_up(kind).wait_recv()

    def lane_of(shape):
        return lax.broadcasted_iota(jnp.int32, shape, 1)

    def exchange(source, target, s_sem, r_sem, c):
        def one(i, carry):
            q = peer(jnp.where(i <= parts // 2, parts // 2 + i - 1, parts - i))
            pltpu.make_async_remote_copy(
                src_ref=source.at[c, q],
                dst_ref=target.at[c, me],
                send_sem=s_sem.at[c],
                recv_sem=r_sem.at[c],
                device_id={"hor": q},
                device_id_type=MESH,
            ).start()
            return carry

        lax.fori_loop(1, parts, one, 0)
        target[c, me] = source[c, me]

    def wait_all(ref, sem, c):
        view = ref.at[c, pl.ds(0, parts - 1)]
        pltpu.make_async_copy(view, view, sem.at[c]).wait()

    def north(c):
        level = pl.ds(c * pack, pack)
        x = jnp.concatenate(
            [field[f, level].reshape(pack * rows, length_y) for f in range(2)], axis=0
        )
        a, b = x[:, :half_y], x[:, half_y:]
        spectra = [
            dot(split3(a + b, 1), fwd_y[0]).reshape(2, pack, rows, half_y),
            dot(split3(a - b, 1), fwd_y[1]).reshape(2, pack, rows, half_y),
        ]
        lane = lane_of((rows, LANES))
        for parity in range(2):
            for tile in range(half_y // LANES):
                q0 = (parity * (half_y // LANES) + tile) * pack
                cols = slice(tile * LANES, (tile + 1) * LANES)
                for f in range(2):
                    tiles = [spectra[parity][f, z, :, cols] for z in range(pack)]
                    for i, t in enumerate(block_transpose(tiles, slots, lane)):
                        send[c, q0 + i, f] = t

    def east(c):
        both = jnp.concatenate(
            [recv[c, :, f].reshape(length_x, LANES) for f in range(2)], axis=1
        )
        a, b = both[:half_x], both[half_x:]
        block = lane_of((1, LANES)) // slots
        rates = []
        for ref in (rate_t, rate_s, rate_c):
            row = jnp.full((1, LANES), ref[c * pack], jnp.float32)
            for z in range(1, pack):
                row = jnp.where(block == z, ref[c * pack + z], row)
            rates.append(row)
        waves_y = wy2[me]
        result = []
        for parity, x in enumerate((a + b, a - b)):
            spec = dot(fwd_x[parity], split3(x, 0))
            t, s = spec[:, :LANES], spec[:, LANES:]
            modulus = wx2[parity] + waves_y
            diag_t = 1.0 + rates[0] * modulus
            diag_s = 1.0 + rates[1] * modulus
            cross = rates[2] * modulus
            inverse = 1.0 / (diag_t * diag_s + cross * cross)
            new = jnp.concatenate(
                [(diag_s * t - cross * s) * inverse, (diag_t * s + cross * t) * inverse], axis=1
            )
            result.append(dot(inv_x[parity], split3(new, 0)))
        for k, x in enumerate((result[0] + result[1], result[0] - result[1])):
            for f in range(2):
                back_send[c, pl.ds(k * (parts // 2), parts // 2), f] = x[
                    :, f * LANES : (f + 1) * LANES
                ].reshape(parts // 2, rows, LANES)

    def south(c):
        lane = lane_of((rows, LANES))
        ends = []
        for parity in range(2):
            fields = []
            columns = []
            for f in range(2):
                by_tile = []
                for tile in range(half_y // LANES):
                    q0 = (parity * (half_y // LANES) + tile) * pack
                    tiles = [back_recv[c, q0 + i, f] for i in range(pack)]
                    by_tile.append(block_transpose(tiles, slots, lane))
                for z in range(pack):
                    columns.append(jnp.concatenate([t[z] for t in by_tile], axis=1))
            x = jnp.concatenate(columns, axis=0)
            ends.append(dot(split3(x, 1), inv_y[parity]))
        for k, x in enumerate((ends[0] + ends[1], ends[0] - ends[1])):
            new[:, pl.ds(c * pack, pack), :, pl.ds(k * half_y, half_y)] = x.reshape(
                2, pack, rows, half_y
            )

    def forward(i):
        c = chunk_of(i)
        field_copy(0, c).wait()
        field_copy(1, c).wait()
        north(c)
        return c

    table_copy(0).wait()
    first = forward(0)
    pl.semaphore_wait(
        barrier, parts - 1 + jnp.where(has_low, 1, 0) + jnp.where(has_high, 1, 0)
    )
    exchange(send, recv, send_sem, recv_sem, first)

    def outward(i, carry):
        exchange(send, recv, send_sem, recv_sem, forward(i))
        return carry

    lax.fori_loop(1, chunks, outward, 0)
    send_halo(0)
    for k in range(1, len(tables)):
        table_copy(k).wait()

    def middle(i, carry):
        c = chunk_of(i)
        wait_all(recv, recv_sem, c)
        east(c)
        exchange(back_send, back_recv, back_send_sem, back_recv_sem, c)
        return carry

    lax.fori_loop(0, chunks, middle, 0)

    def backward(i, carry):
        c = chunk_of(i)
        wait_all(back_recv, back_recv_sem, c)
        south(c)
        new_copy(c).start()
        wait_all(send, send_sem, c)

        @pl.when(i == 1)
        def _():
            send_halo(1)

        return carry

    lax.fori_loop(0, chunks, backward, 0)
    wait_halo(0)
    wait_halo(1)

    def drain(c, carry):
        new_copy(c).wait()
        wait_all(back_send, back_send_sem, c)
        return carry

    lax.fori_loop(0, chunks, drain, 0)


def advect(levs, filtered, speed, speed_ends, out_t, out_s):
    layers = speed.shape[0]
    lev = lax.axis_index("lev")
    r = pl.ds(pl.multiple_of(pl.program_id(0) * 8, 8), 8)

    def level_of(j):
        w = speed_ends[j // (layers + 1), r] if j in (0, layers + 1) else speed[j - 1, r]
        return filtered[0, j, r], filtered[1, j, r], w

    low = level_of(0)
    below = None
    for j in range(layers + 1):
        high = level_of(j + 1)
        flow = 0.5 * (low[2] + high[2]) + buoyancy * 0.5 * (
            (low[0] + high[0]) - (low[1] + high[1])
        )
        up, down = jnp.maximum(flow, 0.0), jnp.minimum(flow, 0.0)
        above = [up * low[f] + down * high[f] for f in range(2)]
        if j == 0:
            above = [jnp.where(lev > 0, x, 0.0) for x in above]
        if j == layers:
            above = [jnp.where(lev < levs - 1, x, 0.0) for x in above]
        if j > 0:
            out_t[j - 1] = low[0] - advective_number * (above[0] - below[0])
            out_s[j - 1] = low[1] - advective_number * (above[1] - below[1])
        low, below = high, above


def shards(heat, salt, speed, rate_t, rate_s, rate_c):
    layers, rows, length_y = heat.shape
    parts = lax.axis_size("hor")
    levs = lax.axis_size("lev")
    length_x = rows * parts
    slots = length_y // parts
    pack = LANES // slots
    chunks = layers // pack
    rows_y, rows_x = basis(length_y), basis(length_x)
    fwd_y = np.stack([thirds(m.T, 0) for m in rows_y])
    inv_y = np.stack([thirds(m, 0) for m in rows_y])
    fwd_x = np.stack([thirds(m, 1) for m in rows_x])
    inv_x = np.stack([thirds(m.T, 1) for m in rows_x])
    scale = (length_x / 2.0) ** 2
    wx2 = np.stack([np.repeat((k * k / scale)[:, None], LANES, 1) for k in wave_table(length_x)])
    every = np.concatenate(wave_table(length_y)).reshape(parts, 1, slots)
    wy2 = np.tile(every * every / scale, (1, 1, pack))
    tables = [jnp.asarray(m) for m in (fwd_y, inv_y, fwd_x, inv_x)]
    tables += [jnp.asarray(m.astype(np.float32)) for m in (wx2, wy2)]
    smem = pl.BlockSpec(memory_space=pltpu.SMEM)
    anywhere = pl.BlockSpec(memory_space=pl.ANY)
    block = pltpu.VMEM((chunks, parts, 2, rows, LANES), jnp.float32)
    sems = pltpu.SemaphoreType.DMA((chunks,))
    whole = pltpu.VMEM((2, layers, rows, length_y), jnp.float32)
    filtered, speed_ends = pl.pallas_call(
        functools.partial(kernel, parts, levs, slots),
        out_shape=(
            pltpu.VMEM((2, layers + 2, rows, length_y), jnp.float32),
            pltpu.VMEM((2, rows, length_y), jnp.float32),
        ),
        in_specs=[anywhere] * 3 + [smem] * 3 + [anywhere] * 6,
        out_specs=(anywhere, anywhere),
        scratch_shapes=[block] * 4
        + [whole] * 2
        + [pltpu.VMEM(t.shape, t.dtype) for t in tables]
        + [sems] * 4
        + [
            pltpu.SemaphoreType.DMA((2, chunks)),
            sems,
            pltpu.SemaphoreType.DMA((len(tables),)),
            pltpu.SemaphoreType.DMA((2, 2)),
            pltpu.SemaphoreType.DMA((2, 2)),
        ],
        compiler_params=pltpu.CompilerParams(
            collective_id=0, has_side_effects=True, vmem_limit_bytes=57 * 2**20
        ),
    )(heat, salt, speed, rate_t, rate_s, rate_c, *tables)
    level = pl.BlockSpec((layers, 8, length_y), lambda i: (0, i, 0))
    whole = pl.BlockSpec(memory_space=pltpu.VMEM)
    shape = jax.ShapeDtypeStruct(heat.shape, jnp.float32)
    return pl.pallas_call(
        functools.partial(advect, levs),
        grid=(rows // 8,),
        out_shape=(shape, shape),
        in_specs=[whole] * 3,
        out_specs=(level, level),
        compiler_params=pltpu.CompilerParams(vmem_limit_bytes=16 * 2**20),
    )(filtered, speed, speed_ends)


def solution(mesh):
    field = P("lev", "hor", None)
    in_specs = (field, field, field, P("lev"), P("lev"), P("lev"))
    return jax.shard_map(
        shards, mesh=mesh, in_specs=in_specs, out_specs=(field, field), check_vma=False
    )
```

```python
import functools
import math

import jax
import jax.numpy as jnp
import ml_dtypes
import numpy as np
from jax import lax
from jax.experimental import pallas as pl
from jax.experimental.pallas import tpu as pltpu
from jax.sharding import PartitionSpec as P

MESH = pl.DeviceIdType.MESH
LANES = 128
buoyancy = 0.5
advective_number = 0.25


def wave_table(length):
    half = length // 2
    waves = []
    for parity in range(2):
        k = np.repeat(2 * np.arange(half // 2) + parity, 2)
        if parity == 0:
            k[1] = half
        waves.append(k)
    return waves


def basis(length):
    half = length // 2
    points = np.arange(half)
    out = []
    for parity, k in enumerate(wave_table(length)):
        angle = 2.0 * math.pi / length * ((k[:, None] * points[None, :]) % length)
        rows = np.where(np.arange(half)[:, None] % 2 == 0, np.cos(angle), np.sin(angle))
        rows = rows * math.sqrt(2.0 / length)
        if parity == 0:
            rows[0] = 1.0 / math.sqrt(length)
            rows[1] = np.cos(math.pi * points) / math.sqrt(length)
        out.append(rows)
    return out


def thirds(matrix, axis):
    high = matrix.astype(ml_dtypes.bfloat16)
    low = (matrix - high.astype(np.float64)).astype(ml_dtypes.bfloat16)
    return np.concatenate([high, high, low], axis=axis)


def split3(x, axis):
    high = x.astype(jnp.bfloat16)
    low = (x - high.astype(jnp.float32)).astype(jnp.bfloat16)
    return jnp.concatenate([high, low, high], axis=axis)


def dot(a, b):
    return jnp.dot(a, b, preferred_element_type=jnp.float32)


def block_transpose(tiles, width, lane):
    count = len(tiles)
    tiles = list(tiles)
    step = count // 2
    while step >= 1:
        keep = (lane // width) % (2 * step) < step
        for i in range(count):
            if i & step == 0:
                a, b = tiles[i], tiles[i + step]
                tiles[i] = jnp.where(keep, a, pltpu.roll(b, step * width, 1))
                tiles[i + step] = jnp.where(
                    keep, pltpu.roll(a, LANES - step * width, 1), b
                )
        step //= 2
    return tiles


def kernel(
    parts, levs, slots,
    heat, salt, speed, rate_t, rate_s, rate_c, *rest
):
    sources, rest = rest[:6], rest[6:]
    filtered, speed_ends = rest[:2]
    send, recv, back_send, back_recv, field, new, *tables = rest[2:14]
    fwd_y, inv_y, fwd_x, inv_x, wx2, wy2 = tables
    send_sem, recv_sem, back_send_sem, back_recv_sem = rest[14:18]
    field_sem, new_sem, table_sem, halo_send, halo_recv = rest[18:]
    layers, rows, length_y = heat.shape
    pack = LANES // slots
    chunks = layers // pack
    half_y = length_y // 2
    length_x = rows * parts
    half_x = length_x // 2
    me = lax.axis_index("hor")
    lev = lax.axis_index("lev")
    has_low = lev > 0
    has_high = lev < levs - 1

    def peer(d):
        return lax.rem(me + d, parts)

    barrier = pltpu.get_barrier_semaphore()

    def greet(d, carry):
        pl.semaphore_signal(barrier, inc=1, device_id={"hor": peer(d)}, device_id_type=MESH)
        return carry

    lax.fori_loop(1, parts, greet, 0)

    @pl.when(has_low)
    def _():
        pl.semaphore_signal(barrier, inc=1, device_id={"lev": lev - 1}, device_id_type=MESH)

    @pl.when(has_high)
    def _():
        pl.semaphore_signal(barrier, inc=1, device_id={"lev": lev + 1}, device_id_type=MESH)

    def field_copy(f, c):
        level = pl.ds(c * pack, pack)
        return pltpu.make_async_copy(
            (heat, salt)[f].at[level], field.at[f, level], field_sem.at[f, c]
        )

    def table_copy(k):
        return pltpu.make_async_copy(sources[k], tables[k], table_sem.at[k])

    def new_copy(c):
        return pltpu.make_async_copy(
            new.at[:, pl.ds(c * pack, pack)],
            filtered.at[:, pl.ds(1 + c * pack, pack)],
            new_sem.at[c],
        )

    def chunk_of(i):
        return lax.rem(i + chunks - 1, chunks)

    def read(i, carry):
        field_copy(0, chunk_of(i)).start()
        field_copy(1, chunk_of(i)).start()
        return carry

    table_copy(0).start()
    lax.fori_loop(0, chunks, read, 0)
    for k in range(1, len(tables)):
        table_copy(k).start()

    def halo(up, kind):
        level, place = (layers - 1, 0) if up else (0, 1)
        if kind == 0:
            source, target = speed.at[level], speed_ends.at[place]
        else:
            source, target = new.at[:, level], filtered.at[:, place * (layers + 1)]
        way = 0 if up else 1
        return pltpu.make_async_remote_copy(
            src_ref=source,
            dst_ref=target,
            send_sem=halo_send.at[way, kind],
            recv_sem=halo_recv.at[way, kind],
            device_id={"lev": lev + 1 if up else lev - 1},
            device_id_type=MESH,
        )

    halo_up = functools.partial(halo, True)
    halo_down = functools.partial(halo, False)

    def send_halo(kind):
        @pl.when(has_high)
        def _():
            halo_up(kind).start()

        @pl.when(has_low)
        def _():
            halo_down(kind).start()

    def wait_halo(kind):
        @pl.when(has_high)
        def _():
            halo_up(kind).wait_send()
            halo_down(kind).wait_recv()

        @pl.when(has_low)
        def _():
            halo_down(kind).wait_send()
            halo_up(kind).wait_recv()

    def lane_of(shape):
        return lax.broadcasted_iota(jnp.int32, shape, 1)

    def exchange(source, target, s_sem, r_sem, c):
        def one(d, carry):
            q = peer(parts - d)
            pltpu.make_async_remote_copy(
                src_ref=source.at[c, q],
                dst_ref=target.at[c, me],
                send_sem=s_sem.at[c],
                recv_sem=r_sem.at[c],
                device_id={"hor": q},
                device_id_type=MESH,
            ).start()
            return carry

        lax.fori_loop(1, parts, one, 0)
        target[c, me] = source[c, me]

    def wait_all(ref, sem, c):
        view = ref.at[c, pl.ds(0, parts - 1)]
        pltpu.make_async_copy(view, view, sem.at[c]).wait()

    def north(c):
        level = pl.ds(c * pack, pack)
        x = jnp.concatenate(
            [field[f, level].reshape(pack * rows, length_y) for f in range(2)], axis=0
        )
        a, b = x[:, :half_y], x[:, half_y:]
        spectra = [
            dot(split3(a + b, 1), fwd_y[0]).reshape(2, pack, rows, half_y),
            dot(split3(a - b, 1), fwd_y[1]).reshape(2, pack, rows, half_y),
        ]
        lane = lane_of((rows, LANES))
        for parity in range(2):
            for tile in range(half_y // LANES):
                q0 = (parity * (half_y // LANES) + tile) * pack
                cols = slice(tile * LANES, (tile + 1) * LANES)
                for f in range(2):
                    tiles = [spectra[parity][f, z, :, cols] for z in range(pack)]
                    for i, t in enumerate(block_transpose(tiles, slots, lane)):
                        send[c, q0 + i, f] = t

    def east(c):
        both = jnp.concatenate(
            [recv[c, :, f].reshape(length_x, LANES) for f in range(2)], axis=1
        )
        a, b = both[:half_x], both[half_x:]
        block = lane_of((1, LANES)) // slots
        rates = []
        for ref in (rate_t, rate_s, rate_c):
            row = jnp.full((1, LANES), ref[c * pack], jnp.float32)
            for z in range(1, pack):
                row = jnp.where(block == z, ref[c * pack + z], row)
            rates.append(row)
        waves_y = wy2[me]
        result = []
        for parity, x in enumerate((a + b, a - b)):
            spec = dot(fwd_x[parity], split3(x, 0))
            t, s = spec[:, :LANES], spec[:, LANES:]
            modulus = wx2[parity] + waves_y
            diag_t = 1.0 + rates[0] * modulus
            diag_s = 1.0 + rates[1] * modulus
            cross = rates[2] * modulus
            inverse = 1.0 / (diag_t * diag_s + cross * cross)
            new = jnp.concatenate(
                [(diag_s * t - cross * s) * inverse, (diag_t * s + cross * t) * inverse], axis=1
            )
            result.append(dot(inv_x[parity], split3(new, 0)))
        for k, x in enumerate((result[0] + result[1], result[0] - result[1])):
            for f in range(2):
                back_send[c, pl.ds(k * (parts // 2), parts // 2), f] = x[
                    :, f * LANES : (f + 1) * LANES
                ].reshape(parts // 2, rows, LANES)

    def south(c):
        lane = lane_of((rows, LANES))
        ends = []
        for parity in range(2):
            fields = []
            columns = []
            for f in range(2):
                by_tile = []
                for tile in range(half_y // LANES):
                    q0 = (parity * (half_y // LANES) + tile) * pack
                    tiles = [back_recv[c, q0 + i, f] for i in range(pack)]
                    by_tile.append(block_transpose(tiles, slots, lane))
                for z in range(pack):
                    columns.append(jnp.concatenate([t[z] for t in by_tile], axis=1))
            x = jnp.concatenate(columns, axis=0)
            ends.append(dot(split3(x, 1), inv_y[parity]))
        for k, x in enumerate((ends[0] + ends[1], ends[0] - ends[1])):
            new[:, pl.ds(c * pack, pack), :, pl.ds(k * half_y, half_y)] = x.reshape(
                2, pack, rows, half_y
            )

    def forward(i):
        c = chunk_of(i)
        field_copy(0, c).wait()
        field_copy(1, c).wait()
        north(c)
        return c

    table_copy(0).wait()
    first = forward(0)
    pl.semaphore_wait(
        barrier, parts - 1 + jnp.where(has_low, 1, 0) + jnp.where(has_high, 1, 0)
    )
    exchange(send, recv, send_sem, recv_sem, first)

    def outward(i, carry):
        exchange(send, recv, send_sem, recv_sem, forward(i))
        return carry

    lax.fori_loop(1, chunks, outward, 0)
    send_halo(0)
    for k in range(1, len(tables)):
        table_copy(k).wait()

    def middle(i, carry):
        c = chunk_of(i)
        wait_all(recv, recv_sem, c)
        east(c)
        exchange(back_send, back_recv, back_send_sem, back_recv_sem, c)
        return carry

    lax.fori_loop(0, chunks, middle, 0)

    def backward(i, carry):
        c = chunk_of(i)
        wait_all(back_recv, back_recv_sem, c)
        south(c)
        new_copy(c).start()

        @pl.when(i == 1)
        def _():
            send_halo(1)

        return carry

    lax.fori_loop(0, chunks, backward, 0)
    wait_halo(0)
    wait_halo(1)

    def drain(c, carry):
        new_copy(c).wait()
        wait_all(send, send_sem, c)
        wait_all(back_send, back_send_sem, c)
        return carry

    lax.fori_loop(0, chunks, drain, 0)


def advect(levs, filtered, speed, speed_ends, out_t, out_s):
    layers = speed.shape[0]
    lev = lax.axis_index("lev")
    r = pl.ds(pl.multiple_of(pl.program_id(0) * 8, 8), 8)

    def level_of(j):
        w = speed_ends[j // (layers + 1), r] if j in (0, layers + 1) else speed[j - 1, r]
        return filtered[0, j, r], filtered[1, j, r], w

    low = level_of(0)
    below = None
    for j in range(layers + 1):
        high = level_of(j + 1)
        flow = 0.5 * (low[2] + high[2]) + buoyancy * 0.5 * (
            (low[0] + high[0]) - (low[1] + high[1])
        )
        up, down = jnp.maximum(flow, 0.0), jnp.minimum(flow, 0.0)
        above = [up * low[f] + down * high[f] for f in range(2)]
        if j == 0:
            above = [jnp.where(lev > 0, x, 0.0) for x in above]
        if j == layers:
            above = [jnp.where(lev < levs - 1, x, 0.0) for x in above]
        if j > 0:
            out_t[j - 1] = low[0] - advective_number * (above[0] - below[0])
            out_s[j - 1] = low[1] - advective_number * (above[1] - below[1])
        low, below = high, above


def shards(heat, salt, speed, rate_t, rate_s, rate_c):
    layers, rows, length_y = heat.shape
    parts = lax.axis_size("hor")
    levs = lax.axis_size("lev")
    length_x = rows * parts
    slots = length_y // parts
    pack = LANES // slots
    chunks = layers // pack
    rows_y, rows_x = basis(length_y), basis(length_x)
    fwd_y = np.stack([thirds(m.T, 0) for m in rows_y])
    inv_y = np.stack([thirds(m, 0) for m in rows_y])
    fwd_x = np.stack([thirds(m, 1) for m in rows_x])
    inv_x = np.stack([thirds(m.T, 1) for m in rows_x])
    scale = (length_x / 2.0) ** 2
    wx2 = np.stack([np.repeat((k * k / scale)[:, None], LANES, 1) for k in wave_table(length_x)])
    every = np.concatenate(wave_table(length_y)).reshape(parts, 1, slots)
    wy2 = np.tile(every * every / scale, (1, 1, pack))
    tables = [jnp.asarray(m) for m in (fwd_y, inv_y, fwd_x, inv_x)]
    tables += [jnp.asarray(m.astype(np.float32)) for m in (wx2, wy2)]
    smem = pl.BlockSpec(memory_space=pltpu.SMEM)
    anywhere = pl.BlockSpec(memory_space=pl.ANY)
    block = pltpu.VMEM((chunks, parts, 2, rows, LANES), jnp.float32)
    sems = pltpu.SemaphoreType.DMA((chunks,))
    whole = pltpu.VMEM((2, layers, rows, length_y), jnp.float32)
    filtered, speed_ends = pl.pallas_call(
        functools.partial(kernel, parts, levs, slots),
        out_shape=(
            pltpu.VMEM((2, layers + 2, rows, length_y), jnp.float32),
            pltpu.VMEM((2, rows, length_y), jnp.float32),
        ),
        in_specs=[anywhere] * 3 + [smem] * 3 + [anywhere] * 6,
        out_specs=(anywhere, anywhere),
        scratch_shapes=[block] * 4
        + [whole] * 2
        + [pltpu.VMEM(t.shape, t.dtype) for t in tables]
        + [sems] * 4
        + [
            pltpu.SemaphoreType.DMA((2, chunks)),
            sems,
            pltpu.SemaphoreType.DMA((len(tables),)),
            pltpu.SemaphoreType.DMA((2, 2)),
            pltpu.SemaphoreType.DMA((2, 2)),
        ],
        compiler_params=pltpu.CompilerParams(
            collective_id=0, has_side_effects=True, vmem_limit_bytes=57 * 2**20
        ),
    )(heat, salt, speed, rate_t, rate_s, rate_c, *tables)
    level = pl.BlockSpec((layers, 8, length_y), lambda i: (0, i, 0))
    whole = pl.BlockSpec(memory_space=pltpu.VMEM)
    shape = jax.ShapeDtypeStruct(heat.shape, jnp.float32)
    return pl.pallas_call(
        functools.partial(advect, levs),
        grid=(rows // 8,),
        out_shape=(shape, shape),
        in_specs=[whole] * 3,
        out_specs=(level, level),
        compiler_params=pltpu.CompilerParams(vmem_limit_bytes=16 * 2**20),
    )(filtered, speed, speed_ends)


def solution(mesh):
    field = P("lev", "hor", None)
    in_specs = (field, field, field, P("lev"), P("lev"), P("lev"))
    return jax.shard_map(
        shards, mesh=mesh, in_specs=in_specs, out_specs=(field, field), check_vma=False
    )
```
